32 devices in a mesh: erow: 4 (over x, core), ecol: 8 (over z, y).
Axes of the slice: x: 2, y: 2, z: 4, core: 2. Of those that a mesh axis runs over, the one named last changes fastest.
Arguments:
- tokens: bfloat16 [256, 7168], P(('erow', 'ecol')), may hold values from -6 to 6
- routes: int32 [256, 4], P(('erow', 'ecol')), may hold values from 0 to 7, all different within a row; in each aligned block of 8 rows (0 to 7, 8 to 15, ...) at most 4 rows name the same one
- gate_probs: bfloat16 [256, 4], P(('erow', 'ecol')), may hold values from 0.049804688 to 0.5
- cotangent: bfloat16 [256, 7168], P(('erow', 'ecol')), may hold values from -0.625 to 0.625
- w_gate_up: bfloat16 [8, 7168, 2, 2048], P('ecol', 'erow'), may hold values from -0.0625 to 0.0625
- w_down: bfloat16 [8, 2048, 7168], P('ecol', None, 'erow'), may hold values from -0.125 to 0.125
Outputs:
- layer_out: bfloat16 [256, 7168], P(('erow', 'ecol'))
- grad_tokens: bfloat16 [256, 7168], P(('erow', 'ecol'))
- grad_probs: float32 [256, 4], P(('erow', 'ecol'))
- grad_gate_up: bfloat16 [8, 7168, 2, 2048], P('ecol', 'erow')
- grad_down: bfloat16 [8, 2048, 7168], P('ecol', None, 'erow')
The draws below stay inside these ranges and needn't reach their ends.
Inputs may be any that keep to these rules, and one draw needn't show every extreme that they name: `routes`: each row names 4 different experts; among the 8 rows of one device no expert is named more than 4 times, and in some device's rows an expert is named exactly 4 times.
All inputs are finite; a program needn't handle non-finite values.
Results may differ from the reference program's by a relative error of at most 0.039.
Values may be sent and summed in bfloat16 or wider, within the bound.
No kernel may reach another device: no remote copies, remote signals or barrier semaphores. Data moves between devices by JAX's collectives and lax.ppermute only.
A program may use at most 128 MiB of HBM per device.

```python
import math
import jax
import jax.numpy as jnp
import numpy as np
from jax import lax

D = 7168
EXPERT_HIDDEN = 2048
TOP_W = 4
TOK_DEV = 8
CAP = 4
EXPERTS = 8
TOKENS = 256
N_EROW = 4


def block_levels(own_key, shape, shards, smallest, largest):
    level, own = 1.0, jax.random.fold_in(own_key, 6)
    for dim, blocks in shards:
        steps = jnp.exp(jax.random.uniform(jax.random.fold_in(own, dim), (blocks,), jnp.float32, smallest / len(shards), largest / len(shards)))
        level = level * jnp.repeat(steps, shape[dim] // blocks).reshape([-1 if axis == dim else 1 for axis in range(len(shape))])
    return level


def shared_out(own_key, own, number, rows, count, top, limit, slope):
    sequence = jax.random.permutation(own_key, count)
    heavy_load, common = portions_of(count, rows * top, limit, slope, True), portions_of(count, rows * top, limit, slope, False)
    places = jnp.arange(count)

    def named(tallies, turn):
        used = int((tallies > 0).sum())
        fixed = max(1, used // 4)
        moved = fixed + (places - fixed + turn * (used - fixed)) % max(1, count - fixed)
        return jnp.zeros((count,), jnp.int32).at[sequence[jnp.where(places < fixed, places, moved)]].set(jnp.asarray(tallies, jnp.int32))

    tallies = jnp.where(number % 4 == 0, named(heavy_load, number // 4), named(common, number - number // 4 - 1))
    mixed = jax.random.permutation(jax.random.fold_in(own, 3), count)
    donor, taker = mixed[0:count // 2 * 2:2], mixed[1:count // 2 * 2:2]
    margin = jnp.minimum(tallies[donor] - 1, limit - tallies[taker]) // 2
    margin = jnp.where((donor == sequence[0]) | (taker == sequence[0]) | (tallies[taker] == 0), 0, jnp.maximum(margin, 0))
    moved = jax.random.randint(jax.random.fold_in(own, 4), (count // 2,), 0, 1 << 20) % (margin + 1)
    tallies = tallies.at[donor].add(-moved).at[taker].add(moved)
    members = jnp.searchsorted(jnp.cumsum(tallies), jnp.arange(rows * top), side="right").astype(jnp.int32)
    table = members.reshape(top, rows).T
    table = table[jax.random.permutation(jax.random.fold_in(own, 1), rows)]
    turn = jax.random.randint(jax.random.fold_in(own, 2), (rows, 1), 0, top)
    return jnp.take_along_axis(table, (jnp.arange(top)[None, :] + turn) % top, axis=1)


def portions_of(number_of, total, bound, skew, full):
    portions = [(1 << 20) // math.isqrt(rank ** skew) + 1 for rank in range(1, number_of + 1)]
    largest = bound if full else min(bound, max(-(-total // number_of), total * portions[0] // sum(portions)))
    least = 1 if total - largest >= number_of - 1 else 0
    given, surplus = [largest] + [least] * (number_of - 1), total - largest - least * (number_of - 1)
    while surplus > 0:
        free = [i for i in range(1, number_of) if given[i] < largest] or [i for i in range(1, number_of) if given[i] < bound]
        whole, budget = sum([portions[i] for i in free]), surplus
        for i in free:
            more = min(bound - given[i], max(1, budget * portions[i] // whole), surplus)
            given[i] = given[i] + more
            surplus = surplus - more
    return np.array(given)


def gaussian(own_key, extent, deviation, most, shards=(), kind=jnp.bfloat16):
    values = deviation * jax.random.normal(own_key, extent, jnp.float32)
    if shards:
        values = values * block_levels(own_key, extent, shards, -0.22, 0.18)
    return jnp.clip(values, -most, most).astype(kind)


def setup_inputs(seed: int = 0) -> dict:
    key_list = jax.random.split(jax.random.key(seed), 7)
    tokens = gaussian(key_list[0], (TOKENS, D), 1.0, 6.0, ((0, 32),))
    routes_keys = jax.random.split(jax.random.fold_in(key_list[1], 1), TOKENS // TOK_DEV)
    routes_turns = jax.random.permutation(jax.random.fold_in(key_list[1], 3), TOKENS // TOK_DEV)
    routes = jax.vmap(lambda own, number: shared_out(jax.random.fold_in(key_list[1], 2), own, number, TOK_DEV, EXPERTS, TOP_W, CAP, 2))(routes_keys, routes_turns).reshape((TOKENS, TOP_W))
    gate_probs = jnp.clip(jnp.exp(math.log(0.5) - 2.306499 * jax.random.uniform(key_list[2], (TOKENS, TOP_W), jnp.float32) ** block_levels(key_list[2], (TOKENS, TOP_W), ((0, 32),), -0.2, 0.2)), 0.049804688, 0.5).astype(jnp.bfloat16)
    cotangent = gaussian(key_list[3], (TOKENS, D), 0.1, 0.625, ((0, 32),))
    w_gate_up = gaussian(key_list[4], (EXPERTS, D, 2, EXPERT_HIDDEN), D ** -0.5, 0.0625, ((0, 8), (1, 4)))
    w_down = gaussian(key_list[5], (EXPERTS, EXPERT_HIDDEN, D), EXPERT_HIDDEN ** -0.5, 0.125, ((0, 8), (2, 4)))
    return dict(tokens=tokens, routes=routes, gate_probs=gate_probs, cotangent=cotangent, w_gate_up=w_gate_up, w_down=w_down)


def rounded(value):
    return lax.optimization_barrier(value.astype(jnp.bfloat16)).astype(jnp.float32)


def reference(tokens, routes, gate_probs, cotangent, w_gate_up, w_down):
    token_count = tokens.shape[0]
    model_width = tokens.shape[1]
    weight_slice = model_width // N_EROW
    expert_ids = jnp.arange(EXPERTS, dtype=jnp.int32)
    chosen = routes[:, :, None] == expert_ids[None, None, :]
    probs_te = jnp.sum(jnp.where(chosen, gate_probs.astype(jnp.float32)[:, :, None], 0.0), axis=1)
    tokens_f = tokens.astype(jnp.float32)
    token_blocks = tokens_f.reshape(token_count, N_EROW, weight_slice)
    cot_f32 = cotangent.astype(jnp.float32)
    cot_blocks = cot_f32.reshape(token_count, N_EROW, weight_slice)

    def expert_step(totals, inputs):
        out_acc, grad_acc = totals
        w_in, w_out, expert_index = inputs
        prob_col = jnp.sum(jnp.where(expert_ids[None, :] == expert_index, probs_te, 0.0), axis=1)
        w_in_f = w_in.astype(jnp.float32)
        output_weight_float = w_out.astype(jnp.float32)
        parts = jnp.einsum("trd,rdgf->trgf", token_blocks, w_in_f.reshape(N_EROW, weight_slice, 2, EXPERT_HIDDEN))
        pre_sums = jnp.sum(rounded(parts), axis=1)
        gate_pre = pre_sums[:, 0, :]
        up_pre = pre_sums[:, 1, :]
        sigmoid_gate = jax.nn.sigmoid(gate_pre)
        activated = gate_pre * sigmoid_gate
        hidden = (activated * up_pre).astype(jnp.bfloat16)
        expert_out = jnp.dot(hidden, w_out, preferred_element_type=jnp.float32)
        out_acc = out_acc + rounded(prob_col[:, None] * expert_out)
        scaled_cotangent = rounded(prob_col[:, None] * cot_f32)
        dot_parts = jnp.sum(cot_blocks * expert_out.reshape(token_count, N_EROW, weight_slice), axis=2)
        dprob = jnp.sum(rounded(dot_parts), axis=1)
        hidden_pieces = jnp.einsum("kxa,hxa->kxh", scaled_cotangent.reshape(token_count, N_EROW, weight_slice), output_weight_float.reshape(EXPERT_HIDDEN, N_EROW, weight_slice))
        hidden_gradient = jnp.sum(rounded(hidden_pieces), axis=1)
        grad_gate = hidden_gradient * up_pre * sigmoid_gate * (1.0 + gate_pre * (1.0 - sigmoid_gate))
        grad_up = hidden_gradient * activated
        grad_pre = rounded(jnp.stack([grad_gate, grad_up], axis=1))
        grad_rows = rounded(jnp.einsum("tgf,dgf->td", grad_pre, w_in_f))
        grad_acc = grad_acc + grad_rows
        grad_in = jnp.einsum("td,tgf->dgf", tokens_f, grad_pre).astype(jnp.bfloat16)
        grad_out = jnp.einsum("tf,td->fd", hidden.astype(jnp.float32), scaled_cotangent).astype(jnp.bfloat16)
        return (out_acc, grad_acc), (dprob, grad_in, grad_out)

    zeros = jnp.zeros((token_count, model_width), jnp.float32)
    totals, stacked = lax.scan(expert_step, (zeros, zeros), (w_gate_up, w_down, expert_ids))
    dprob_all, grad_gate_up, grad_down = stacked
    grad_probs = jnp.sum(jnp.where(chosen, jnp.transpose(dprob_all)[:, None, :], 0.0), axis=2)
    return (totals[0].astype(jnp.bfloat16), totals[1].astype(jnp.bfloat16), grad_probs, grad_gate_up, grad_down)
```

```python
import functools

import jax
import jax.numpy as jnp
from jax import lax
from jax.experimental import pallas as pl
from jax.experimental.pallas import tpu as pltpu
from jax.sharding import PartitionSpec as P

BF16 = jnp.bfloat16
F32 = jnp.float32
BOTH = ("erow", "ecol")
VMEM_LIMIT = 48 * 1024 * 1024


def dot(a, b, ca=1, cb=0):
    return lax.dot_general(a, b, (((ca,), (cb,)), ((), ())), preferred_element_type=F32)


def params():
    return pltpu.CompilerParams(vmem_limit_bytes=VMEM_LIMIT)


def cost(flops, bytes_accessed):
    return pl.CostEstimate(flops=int(flops), bytes_accessed=int(bytes_accessed), transcendentals=0)


def whole(shape):
    return pl.BlockSpec(shape, lambda *_: (0,) * len(shape))


def slots_kernel(experts, capacity, routes_ref, gate_ref, tok_ref, cot_ref, x_ref, sc_ref, place_ref, weight_ref):
    count, top = routes_ref.shape
    slots = experts * capacity
    width = x_ref.shape[2]
    slot = lax.broadcasted_iota(jnp.int32, (count, slots), 1)
    expert, rank = slot // capacity, slot % capacity
    member = jnp.zeros((count, slots), F32)
    prob = jnp.zeros((count, slots), F32)
    for k in range(top):
        hit = routes_ref[:, k : k + 1] == expert
        member = member + jnp.where(hit, 1.0, 0.0)
        prob = prob + jnp.where(hit, gate_ref[:, k : k + 1].astype(F32), 0.0)
    row = lax.broadcasted_iota(jnp.int32, (count, count), 0)
    col = lax.broadcasted_iota(jnp.int32, (count, count), 1)
    earlier = jnp.where(col < row, 1.0, 0.0)
    prior = dot(earlier, member)
    placed = (member > 0.5) & (prior == rank.astype(F32))
    place = jnp.where(placed, 1.0, 0.0).astype(BF16)
    weight = jnp.where(placed, prob, 0.0).astype(BF16)
    place_ref[...] = place
    weight_ref[...] = weight
    for r in range(x_ref.shape[0] // experts):
        span = slice(r * width, (r + 1) * width)
        rows = slice(r * experts, (r + 1) * experts)
        x_ref[rows] = dot(place, tok_ref[:, span], 0, 0).astype(BF16).reshape(experts, capacity, width)
        sc_ref[rows] = dot(weight, cot_ref[:, span], 0, 0).astype(BF16).reshape(experts, capacity, width)


def to_slots(routes, gate_probs, tokens, cotangent, n_row, experts, capacity):
    count, model = tokens.shape
    slots = experts * capacity
    sent = jax.ShapeDtypeStruct((n_row * experts, capacity, model // n_row), BF16)
    table = jax.ShapeDtypeStruct((count, slots), BF16)
    return pl.pallas_call(
        functools.partial(slots_kernel, experts, capacity),
        out_shape=(sent, sent, table, table),
        compiler_params=params(),
        cost_estimate=cost(4 * slots * count * model, 10 * slots * model),
    )(routes, gate_probs, tokens, cotangent)


def exchange(rows):
    return lax.all_to_all(rows, BOTH, split_axis=0, concat_axis=0, tiled=True)


def pre_first_kernel(core_ref, x_ref, w_ref, out_ref, spread_ref):
    @pl.when(pl.program_id(0) == 0)
    def _():
        rows, width = spread_ref.shape[0] // 2, spread_ref.shape[1] // 2
        d = lax.broadcasted_iota(jnp.int32, (128, 256), 0)
        lane = lax.broadcasted_iota(jnp.int32, (128, 256), 1)
        x = x_ref[...].reshape(rows, width)
        for g in range(2):
            spread = jnp.where(lane == 2 * d + g, 1.0, 0.0).astype(BF16)
            for j in range(width // 128):
                part = dot(x[:, j * 128 : (j + 1) * 128], spread).astype(BF16)
                spread_ref[g * rows : (g + 1) * rows, j * 256 : (j + 1) * 256] = part

    w = w_ref[...].reshape(spread_ref.shape[1], w_ref.shape[2])
    out_ref[...] = dot(spread_ref[...], w).astype(out_ref.dtype)


def pre_second_kernel(core_ref, spread_ref, w_ref, out_ref):
    w = w_ref[...].reshape(spread_ref.shape[1], w_ref.shape[2])
    out_ref[...] = dot(spread_ref[...], w).astype(out_ref.dtype)


def pre_halves(core, x_in, w_in, rows):
    width, _, hidden = w_in.shape
    half = hidden // 2
    block = 256
    steps = half // block
    work = cost(8 * rows * width * half, 2 * width * hidden + 4 * rows * width)
    send, spread = pl.pallas_call(
        pre_first_kernel,
        grid_spec=pltpu.PrefetchScalarGridSpec(
            num_scalar_prefetch=1,
            grid=(steps,),
            in_specs=[
                whole(x_in.shape),
                pl.BlockSpec((width, 2, block), lambda i, c: (0, 0, (1 - c[0]) * steps + i)),
            ],
            out_specs=[
                pl.BlockSpec((2 * rows, block), lambda i, c: (0, i)),
                whole((2 * rows, 2 * width)),
            ],
        ),
        out_shape=(
            jax.ShapeDtypeStruct((2 * rows, half), BF16),
            jax.ShapeDtypeStruct((2 * rows, 2 * width), BF16),
        ),
        compiler_params=params(),
        cost_estimate=work,
    )(core, x_in, w_in)
    keep = pl.pallas_call(
        pre_second_kernel,
        grid_spec=pltpu.PrefetchScalarGridSpec(
            num_scalar_prefetch=1,
            grid=(steps,),
            in_specs=[
                whole((2 * rows, 2 * width)),
                pl.BlockSpec((width, 2, block), lambda i, c: (0, 0, c[0] * steps + i)),
            ],
            out_specs=pl.BlockSpec((2 * rows, block), lambda i, c: (0, i)),
        ),
        out_shape=jax.ShapeDtypeStruct((2 * rows, half), F32),
        compiler_params=params(),
        cost_estimate=work,
    )(core, spread, w_in)
    return send, keep, spread


def down_t_kernel(core_ref, sc_ref, w_ref, send_ref, keep_ref):
    sc = sc_ref[...].reshape(send_ref.shape[0], w_ref.shape[1])
    out = dot(sc, w_ref[...], 1, 1)
    step = pl.program_id(0)
    steps = pl.num_programs(0) // 2

    @pl.when(step < steps)
    def _():
        send_ref[...] = out.astype(send_ref.dtype)

    @pl.when(step >= steps)
    def _():
        keep_ref[...] = out


def down_t_halves(core, sc_in, w_out, rows):
    hidden, width = w_out.shape
    half = hidden // 2
    block = 256
    steps = half // block

    def w_index(i, c):
        own = i // steps
        return ((1 - c[0]) * (1 - own) + c[0] * own) * steps + i % steps, 0

    return pl.pallas_call(
        down_t_kernel,
        grid_spec=pltpu.PrefetchScalarGridSpec(
            num_scalar_prefetch=1,
            grid=(2 * steps,),
            in_specs=[whole(sc_in.shape), pl.BlockSpec((block, width), w_index)],
            out_specs=[
                pl.BlockSpec((rows, block), lambda i, c: (0, jnp.minimum(i, steps - 1))),
                pl.BlockSpec((rows, block), lambda i, c: (0, jnp.maximum(i - steps, 0))),
            ],
        ),
        out_shape=(
            jax.ShapeDtypeStruct((rows, half), BF16),
            jax.ShapeDtypeStruct((rows, half), F32),
        ),
        compiler_params=params(),
        cost_estimate=cost(2 * rows * width * hidden, 2 * width * hidden),
    )(core, sc_in, w_out)


def swap_cores(value):
    n_row = lax.axis_size("erow")
    return lax.ppermute(value, "erow", [(i, i ^ 1) for i in range(n_row)])


def sum_parts(send, keep):
    n_row = lax.axis_size("erow")
    pairs = n_row // 2
    chip_sum = (keep + swap_cores(send).astype(F32)).astype(BF16)
    total = chip_sum.astype(F32)
    for k in range(1, pairs):
        perm = [(i, ((i // 2 + k) % pairs) * 2 + i % 2) for i in range(n_row)]
        total = total + lax.ppermute(chip_sum, "erow", perm).astype(F32)
    return total


def expert_out_kernel(core_ref, own_ref, other_ref, w_ref, out_ref):
    half = own_ref.shape[1]
    core = core_ref[0]
    own = w_ref[pl.ds(pl.multiple_of(core * half, half), half), :]
    other = w_ref[pl.ds(pl.multiple_of((1 - core) * half, half), half), :]
    out = dot(own_ref[...], own) + dot(other_ref[...], other)
    out_ref[...] = out.astype(BF16).reshape(out_ref.shape)


def expert_out(core, own, other, w_out, capacity):
    rows, half = own.shape
    hidden, width = w_out.shape
    block = width // 7
    return pl.pallas_call(
        expert_out_kernel,
        grid_spec=pltpu.PrefetchScalarGridSpec(
            num_scalar_prefetch=1,
            grid=(7,),
            in_specs=[
                whole((rows, half)),
                whole((rows, half)),
                pl.BlockSpec((hidden, block), lambda i, c: (0, i)),
            ],
            out_specs=pl.BlockSpec((rows // capacity, capacity, block), lambda i, c: (0, 0, i)),
        ),
        out_shape=jax.ShapeDtypeStruct((rows // capacity, capacity, width), BF16),
        compiler_params=params(),
        cost_estimate=cost(2 * rows * width * hidden, 2 * width * hidden),
    )(core, own, other, w_out)


def join_halves(core_ref, own_ref, other_ref, joined):
    half = own_ref.shape[1]
    core = core_ref[0]
    joined[:, pl.ds(pl.multiple_of(core * half, half), half)] = own_ref[...]
    joined[:, pl.ds(pl.multiple_of((1 - core) * half, half), half)] = other_ref[...]


def grad_rows_kernel(core_ref, own_ref, other_ref, w_ref, out_ref, joined, product):
    @pl.when(pl.program_id(0) == 0)
    def _():
        join_halves(core_ref, own_ref, other_ref, joined)

    block = w_ref.shape[0]
    rows = joined.shape[0] // 2
    w = w_ref[...].reshape(2 * block, joined.shape[1])
    out = dot(w, joined[...], 1, 1)
    chunks = rows // 128
    for j in range(2 * chunks):
        product[j] = out[:, j * 128 : (j + 1) * 128]
    capacity = out_ref.shape[1]
    for j in range(chunks):
        gate = product[j, pl.ds(0, block, stride=2), :]
        up = product[chunks + j, pl.ds(1, block, stride=2), :]
        turned = (gate + up).T.astype(BF16).reshape(128 // capacity, capacity, block)
        out_ref[j * 128 // capacity : (j + 1) * 128 // capacity] = turned


def grad_rows(core, own, other, w_in, capacity):
    rows = own.shape[0] // 2
    width, _, hidden = w_in.shape
    block = width // 7
    return pl.pallas_call(
        grad_rows_kernel,
        grid_spec=pltpu.PrefetchScalarGridSpec(
            num_scalar_prefetch=1,
            grid=(7,),
            in_specs=[
                whole(own.shape),
                whole(own.shape),
                pl.BlockSpec((block, 2, hidden), lambda i, c: (i, 0, 0)),
            ],
            out_specs=pl.BlockSpec((rows // capacity, capacity, block), lambda i, c: (0, 0, i)),
            scratch_shapes=[
                pltpu.VMEM((2 * rows, hidden), BF16),
                pltpu.VMEM((2 * rows // 128, 2 * block, 128), F32),
            ],
        ),
        out_shape=jax.ShapeDtypeStruct((rows // capacity, capacity, width), BF16),
        compiler_params=params(),
        cost_estimate=cost(8 * rows * width * hidden, 4 * width * hidden),
    )(core, own, other, w_in)


def grad_in_kernel(core_ref, own_ref, other_ref, spread_ref, out_ref, joined):
    @pl.when(pl.program_id(0) == 0)
    def _():
        join_halves(core_ref, own_ref, other_ref, joined)

    out = dot(spread_ref[...], joined[...], 0, 0)
    out_ref[...] = out.astype(BF16).reshape(out_ref.shape)


def grad_in(core, own, other, spread):
    both, half = own.shape
    hidden = 2 * half
    width = spread.shape[1] // 2
    block = 128
    return pl.pallas_call(
        grad_in_kernel,
        grid_spec=pltpu.PrefetchScalarGridSpec(
            num_scalar_prefetch=1,
            grid=(width // block,),
            in_specs=[
                whole(own.shape),
                whole(own.shape),
                pl.BlockSpec((both, 2 * block), lambda i, c: (0, i)),
            ],
            out_specs=pl.BlockSpec((block, 2, hidden), lambda i, c: (i, 0, 0)),
            scratch_shapes=[pltpu.VMEM((both, hidden), BF16)],
        ),
        out_shape=jax.ShapeDtypeStruct((width, 2, hidden), BF16),
        compiler_params=params(),
        cost_estimate=cost(4 * both * width * hidden, 4 * width * hidden),
    )(core, own, other, spread)


def grad_out_kernel(core_ref, own_ref, other_ref, sc_ref, out_ref):
    rows = own_ref.shape[0]
    sc = sc_ref[...].reshape(rows, out_ref.shape[1])
    step = pl.program_id(0)
    steps = pl.num_programs(0) // 2

    @pl.when(step < steps)
    def _():
        out_ref[...] = dot(own_ref[...], sc, 0, 0).astype(BF16)

    @pl.when(step >= steps)
    def _():
        out_ref[...] = dot(other_ref[...], sc, 0, 0).astype(BF16)


def grad_out(core, own, other, sc_in):
    rows, half = own.shape
    width = sc_in.shape[2]
    block = 256
    steps = half // block

    def out_index(i, c):
        second = i // steps
        return (c[0] * (1 - second) + (1 - c[0]) * second) * steps + i % steps, 0

    return pl.pallas_call(
        grad_out_kernel,
        grid_spec=pltpu.PrefetchScalarGridSpec(
            num_scalar_prefetch=1,
            grid=(2 * steps,),
            in_specs=[
                pl.BlockSpec((rows, block), lambda i, c: (0, jnp.minimum(i, steps - 1))),
                pl.BlockSpec((rows, block), lambda i, c: (0, jnp.maximum(i - steps, 0))),
                whole(sc_in.shape),
            ],
            out_specs=pl.BlockSpec((block, width), out_index),
        ),
        out_shape=jax.ShapeDtypeStruct((2 * half, width), BF16),
        compiler_params=params(),
        cost_estimate=cost(4 * rows * width * half, 4 * width * half),
    )(core, own, other, sc_in)


def layer_out_kernel(routes_ref, place_ref, weight_ref, cot_ref, rows_ref, out_ref, dprob_ref):
    count, slots = place_ref.shape
    _, capacity, width = rows_ref.shape
    experts = slots // capacity
    dots = jnp.zeros((count, slots), F32)
    for r in range(out_ref.shape[1] // width):
        span = slice(r * width, (r + 1) * width)
        part = rows_ref[r * experts : (r + 1) * experts].reshape(slots, width)
        out_ref[:, span] = dot(weight_ref[...], part).astype(BF16)
        dots = dots + dot(cot_ref[:, span], part, 1, 1)
    dots = jnp.where(place_ref[...].astype(F32) > 0.5, dots, 0.0)
    expert = lax.broadcasted_iota(jnp.int32, (count, slots), 1) // capacity
    column = lax.broadcasted_iota(jnp.int32, dprob_ref.shape, 1)
    grads = jnp.zeros(dprob_ref.shape, F32)
    for k in range(dprob_ref.shape[1]):
        term = jnp.sum(jnp.where(routes_ref[:, k : k + 1] == expert, dots, 0.0), axis=1, keepdims=True)
        grads = grads + jnp.where(column == k, term, 0.0)
    dprob_ref[...] = grads


def layer_out(routes, place, weight, cotangent, returned):
    return pl.pallas_call(
        layer_out_kernel,
        out_shape=(
            jax.ShapeDtypeStruct(cotangent.shape, BF16),
            jax.ShapeDtypeStruct(routes.shape, F32),
        ),
        compiler_params=params(),
        cost_estimate=cost(4 * returned.size * 8, 2 * returned.size),
    )(routes, place, weight, cotangent, returned)


def token_grads_kernel(place_ref, rows_ref, out_ref):
    slots = place_ref.shape[1]
    _, capacity, width = rows_ref.shape
    experts = slots // capacity
    for r in range(out_ref.shape[1] // width):
        part = rows_ref[r * experts : (r + 1) * experts].reshape(slots, width)
        out_ref[:, r * width : (r + 1) * width] = dot(place_ref[...], part).astype(BF16)


def token_grads(place, returned, model):
    return pl.pallas_call(
        token_grads_kernel,
        out_shape=jax.ShapeDtypeStruct((place.shape[0], model), BF16),
        compiler_params=params(),
        cost_estimate=cost(2 * returned.size * 8, 2 * returned.size),
    )(place, returned)


def on_device(tokens, routes, gate_probs, cotangent, w_gate_up, w_down):
    n_row = lax.axis_size("erow")
    experts = lax.axis_size("ecol")
    count, model = tokens.shape
    capacity = count // 2
    rows = n_row * experts * capacity
    core = (lax.axis_index("erow") % 2).astype(jnp.int32).reshape(1)
    w_in = w_gate_up[0]
    w_out = w_down[0]

    x_out, sc_out, place, weight = to_slots(
        routes, gate_probs, tokens, cotangent, n_row, experts, capacity
    )
    x_in = exchange(x_out)
    sc_in = exchange(sc_out)

    pre_send, pre_keep, spread = pre_halves(core, x_in, w_in, rows)
    pre = sum_parts(pre_send, pre_keep)
    gate, up = pre[:rows], pre[rows:]
    s = jax.nn.sigmoid(gate)
    activated = gate * s
    hidden_own = (activated * up).astype(BF16)
    hidden_other = swap_cores(hidden_own)
    out_rows = expert_out(core, hidden_own, hidden_other, w_out, capacity)
    out_back = exchange(out_rows)

    hid_send, hid_keep = down_t_halves(core, sc_in, w_out, rows)
    grad_hidden = sum_parts(hid_send, hid_keep)
    grad_gate = grad_hidden * up * s * (1.0 + gate * (1.0 - s))
    grad_up = grad_hidden * activated
    grad_own = jnp.concatenate([grad_gate, grad_up], axis=0).astype(BF16)
    grad_other = swap_cores(grad_own)
    back_rows = grad_rows(core, grad_own, grad_other, w_in, capacity)
    grad_back = exchange(back_rows)

    grad_down = grad_out(core, hidden_own, hidden_other, sc_in)[None]
    grad_gate_up = grad_in(core, grad_own, grad_other, spread)[None]
    out, grad_probs = layer_out(routes, place, weight, cotangent, out_back)
    grad_tokens = token_grads(place, grad_back, model)
    return (out, grad_tokens, grad_probs, grad_gate_up, grad_down)


def solution(mesh):
    flat = P(BOTH, None)
    return jax.shard_map(
        on_device,
        mesh=mesh,
        in_specs=(flat, flat, flat, flat, P("ecol", "erow", None, None), P("ecol", None, "erow")),
        out_specs=(flat, flat, flat, P("ecol", "erow", None, None), P("ecol", None, "erow")),
        check_vma=False,
    )
```

```python
import functools

import jax
import jax.numpy as jnp
from jax import lax
from jax.experimental import pallas as pl
from jax.experimental.pallas import tpu as pltpu
from jax.sharding import PartitionSpec as P

BF16 = jnp.bfloat16
F32 = jnp.float32
BOTH = ("erow", "ecol")
MIB = 1024 * 1024
HBM = pl.BlockSpec(memory_space=pltpu.HBM)
VMEM = pl.BlockSpec(memory_space=pltpu.VMEM)
SMEM = pl.BlockSpec(memory_space=pltpu.SMEM)


def dot(a, b, ca=1, cb=0):
    return lax.dot_general(a, b, (((ca,), (cb,)), ((), ())), preferred_element_type=F32)


def params(mib):
    return pltpu.CompilerParams(vmem_limit_bytes=mib * MIB)


def cost(flops, bytes_accessed):
    return pl.CostEstimate(flops=int(flops), bytes_accessed=int(bytes_accessed), transcendentals=0)


def in_hbm(array):
    return pltpu.with_memory_space_constraint(array, pltpu.HBM)


def shape(*dims, dtype=BF16):
    return jax.ShapeDtypeStruct(dims, dtype)


def aligned(value, step):
    return pl.multiple_of(value * step, step)


def slot_tables(routes_ref, gate_ref, experts, capacity, group=1):
    top, count = routes_ref.shape
    dims = (experts * group * capacity, count)
    slot = lax.broadcasted_iota(jnp.int32, dims, 0)
    expert, rank = slot // (group * capacity), slot % capacity
    member = jnp.zeros(dims, F32)
    prob = jnp.zeros(dims, F32)
    for k in range(top):
        hit = routes_ref[k : k + 1, :] == expert
        member = member + jnp.where(hit, 1.0, 0.0)
        prob = prob + jnp.where(hit, gate_ref[k : k + 1, :].astype(F32), 0.0)
    before = lax.broadcasted_iota(jnp.int32, (count, count), 0)
    after = lax.broadcasted_iota(jnp.int32, (count, count), 1)
    prior = dot(member, jnp.where(before < after, 1.0, 0.0))
    placed = (member > 0.5) & (prior == rank.astype(F32))
    return placed, prob


def slots_kernel(experts, capacity, weighted, routes_hbm, gate_hbm, rows_hbm, out_ref, routes_ref, gate_ref, rows, sems):
    loads = [
        pltpu.make_async_copy(source, target, sems.at[i])
        for i, (source, target) in enumerate(
            ((routes_hbm, routes_ref), (gate_hbm, gate_ref), (rows_hbm, rows))
        )
    ]
    for load in loads:
        load.start()
    loads[0].wait()
    loads[1].wait()
    placed, prob = slot_tables(routes_ref, gate_ref, experts, capacity)
    table = jnp.where(placed, prob if weighted else 1.0, 0.0).astype(BF16)
    loads[2].wait()
    width = out_ref.shape[2]
    for r in range(out_ref.shape[0] // experts):
        part = dot(table, rows[:, r * width : (r + 1) * width]).astype(BF16)
        out_ref[r * experts : (r + 1) * experts] = part.reshape(experts, capacity, width)


def to_slots(routes, gate_probs, rows, weighted, n_row, experts, capacity):
    count, model = rows.shape
    return pl.pallas_call(
        functools.partial(slots_kernel, experts, capacity, weighted),
        in_specs=[HBM, HBM, HBM],
        out_shape=shape(n_row * experts, capacity, model // n_row),
        scratch_shapes=[
            pltpu.VMEM(routes.shape, routes.dtype),
            pltpu.VMEM(gate_probs.shape, BF16),
            pltpu.VMEM(rows.shape, BF16),
            pltpu.SemaphoreType.DMA((3,)),
        ],
        compiler_params=params(8),
        cost_estimate=cost(2 * experts * capacity * count * model, 2 * rows.size),
    )(in_hbm(routes), in_hbm(gate_probs), in_hbm(rows))


def exchange(rows):
    return lax.all_to_all(rows, BOTH, split_axis=0, concat_axis=0, tiled=True)


def stream(copies, ahead=2):
    for copy in copies[:ahead]:
        copy.start()

    def block(i):
        copies[i].wait()
        if i + ahead < len(copies):
            copies[i + ahead].start()

    return block


def spread_rows(x, spread_ref):
    rows, width = x.shape
    d = lax.broadcasted_iota(jnp.int32, (128, 256), 0)
    lane = lax.broadcasted_iota(jnp.int32, (128, 256), 1)
    for g in range(2):
        pattern = jnp.where(lane == 2 * d + g, 1.0, 0.0).astype(BF16)
        for j in range(width // 128):
            part = dot(x[:, j * 128 : (j + 1) * 128], pattern).astype(BF16)
            spread_ref[g * rows : (g + 1) * rows, j * 256 : (j + 1) * 256] = part


def pre_kernel(core_ref, x_ref, w_hbm, send_ref, keep_ref, spread_ref, buffer, sems):
    steps, width, _, block = buffer.shape
    each = steps // 2

    def copy(i):
        part = 1 - core_ref[0] if i < each else core_ref[0]
        source = w_hbm.at[:, :, pl.ds(aligned(part * each + i % each, block), block)]
        return pltpu.make_async_copy(source, buffer.at[i], sems.at[i])

    ready = stream([copy(i) for i in range(steps)])
    spread_rows(x_ref[...].reshape(spread_ref.shape[0] // 2, width), spread_ref)
    for i in range(steps):
        ready(i)
        out_ref = send_ref if i < each else keep_ref
        out = dot(spread_ref[...], buffer[i].reshape(2 * width, block))
        out_ref[:, i % each * block : (i % each + 1) * block] = out.astype(out_ref.dtype)


def pre_halves(core, x_in, w_in, rows):
    width, _, hidden = w_in.shape
    half = hidden // 2
    steps = 4
    return pl.pallas_call(
        pre_kernel,
        in_specs=[SMEM, VMEM, HBM],
        out_specs=[VMEM, VMEM, VMEM],
        out_shape=(
            shape(2 * rows, half),
            shape(2 * rows, half, dtype=F32),
            shape(2 * rows, 2 * width),
        ),
        scratch_shapes=[
            pltpu.VMEM((steps, width, 2, hidden // steps), BF16),
            pltpu.SemaphoreType.DMA((steps,)),
        ],
        compiler_params=params(28),
        cost_estimate=cost(1e10, 4 * width * hidden),
    )(core, x_in, in_hbm(w_in))


def down_t_kernel(core_ref, sc_ref, w_hbm, send_ref, keep_ref, buffer, sems):
    steps, block, width = buffer.shape
    each = steps // 2

    def copy(i):
        part = 1 - core_ref[0] if i < each else core_ref[0]
        source = w_hbm.at[pl.ds(aligned(part * each + i % each, block), block), :]
        return pltpu.make_async_copy(source, buffer.at[i], sems.at[i])

    ready = stream([copy(i) for i in range(steps)])
    sc = sc_ref[...].reshape(send_ref.shape[0], width)
    for i in range(steps):
        ready(i)
        out_ref = send_ref if i < each else keep_ref
        out = dot(sc, buffer[i], 1, 1)
        out_ref[:, i % each * block : (i % each + 1) * block] = out.astype(out_ref.dtype)


def down_t_halves(core, sc_in, w_out, rows):
    hidden, width = w_out.shape
    half = hidden // 2
    steps = 4
    return pl.pallas_call(
        down_t_kernel,
        in_specs=[SMEM, VMEM, HBM],
        out_specs=[VMEM, VMEM],
        out_shape=(shape(rows, half), shape(rows, half, dtype=F32)),
        scratch_shapes=[
            pltpu.VMEM((steps, hidden // steps, width), BF16),
            pltpu.SemaphoreType.DMA((steps,)),
        ],
        compiler_params=params(16),
        cost_estimate=cost(2 * rows * width * hidden, 2 * width * hidden),
    )(core, sc_in, in_hbm(w_out))


def swap_cores(value):
    n_row = lax.axis_size("erow")
    return lax.ppermute(value, "erow", [(i, i ^ 1) for i in range(n_row)])


def sum_parts(send, keep):
    n_row = lax.axis_size("erow")
    pairs = n_row // 2
    chip_sum = (keep + swap_cores(send).astype(F32)).astype(BF16)
    others = []
    for k in range(1, pairs):
        perm = [(i, ((i // 2 + k) % pairs) * 2 + i % 2) for i in range(n_row)]
        others.append(lax.ppermute(chip_sum, "erow", perm))
    return chip_sum, others


def total(part, others):
    out = part.astype(F32)
    for other in others:
        out = out + other.astype(F32)
    return out


def expert_out_kernel(spans, core_ref, own_ref, other_ref, w_hbm, out_ref, joined, buffer, sems):
    copies = [
        pltpu.make_async_copy(w_hbm.at[:, pl.ds(at, size)], buffer.at[:, pl.ds(at, size)], sems.at[i])
        for i, (at, size) in enumerate(spans)
    ]
    ready = stream(copies)
    join_halves(core_ref, own_ref, other_ref, joined)
    for i, (at, size) in enumerate(spans):
        ready(i)
        out_ref[:, at : at + size] = dot(joined[...], buffer[:, at : at + size]).astype(BF16)


def expert_out(core, own, other, w_out):
    rows, half = own.shape
    hidden, width = w_out.shape
    edges = [width // 128 * i // 4 * 128 for i in range(5)]
    spans = [(at, to - at) for at, to in zip(edges, edges[1:])]
    return pl.pallas_call(
        functools.partial(expert_out_kernel, spans),
        in_specs=[SMEM, VMEM, VMEM, HBM],
        out_specs=VMEM,
        out_shape=shape(rows, width),
        scratch_shapes=[
            pltpu.VMEM((rows, hidden), BF16),
            pltpu.VMEM((hidden, width), BF16),
            pltpu.SemaphoreType.DMA((len(spans),)),
        ],
        compiler_params=params(16),
        cost_estimate=cost(5e9, 2 * width * hidden),
    )(core, own, other, in_hbm(w_out))


def join_halves(core_ref, own_ref, other_ref, joined):
    half = own_ref.shape[1]
    joined[:, pl.ds(aligned(core_ref[0], half), half)] = own_ref[...]
    joined[:, pl.ds(aligned(1 - core_ref[0], half), half)] = other_ref[...]


def grad_rows_kernel(steps, core_ref, own_ref, other_ref, w_ref, eo_ref, out_ref, joined, product):
    join_halves(core_ref, own_ref, other_ref, joined)
    rows = eo_ref.shape[0]
    width, _, hidden = w_ref.shape
    block = width // steps
    capacity = out_ref.shape[1] // 2
    chunks = rows // 128
    for i in range(steps):
        span = slice(i * block, (i + 1) * block)
        out = dot(w_ref[span].reshape(2 * block, hidden), joined[...], 1, 1)
        for j in range(2 * chunks):
            product[i % 2, j] = out[:, j * 128 : (j + 1) * 128]
        for j in range(chunks):
            gate = product[i % 2, j, pl.ds(0, block, stride=2), :]
            up = product[i % 2, chunks + j, pl.ds(1, block, stride=2), :]
            turned = (gate + up).T.astype(BF16).reshape(128 // capacity, capacity, block)
            kept = eo_ref[j * 128 : (j + 1) * 128, span].reshape(128 // capacity, capacity, block)
            both = jnp.concatenate([kept, turned], axis=1)
            out_ref[j * 128 // capacity : (j + 1) * 128 // capacity, :, span] = both


def grad_rows(core, own, other, w_in, out_rows, capacity):
    rows, width = out_rows.shape
    hidden = w_in.shape[2]
    steps = 7
    block = width // steps
    return pl.pallas_call(
        functools.partial(grad_rows_kernel, steps),
        in_specs=[SMEM, VMEM, VMEM, VMEM, VMEM],
        out_specs=VMEM,
        out_shape=shape(rows // capacity, 2 * capacity, width),
        scratch_shapes=[
            pltpu.VMEM((2 * rows, hidden), BF16),
            pltpu.VMEM((2, 2 * rows // 128, 2 * block, 128), F32),
        ],
        compiler_params=params(16),
        cost_estimate=cost(8 * rows * width * hidden, 4 * width * hidden),
    )(core, own, other, w_in, out_rows)


def write_blocks(buffer, sems, make, target):
    steps = buffer.shape[0]

    def copy(i):
        return pltpu.make_async_copy(buffer.at[i], target(i), sems.at[i])

    @pl.loop(0, steps)
    def _(i):
        buffer[i] = make(i)
        copy(i).start()

    @pl.loop(0, steps)
    def _(i):
        copy(i).wait()


def grad_in_kernel(core_ref, own_ref, other_ref, spread_ref, out_hbm, joined, buffer, sems):
    join_halves(core_ref, own_ref, other_ref, joined)
    block = buffer.shape[1]

    def make(i):
        part = spread_ref[:, pl.ds(aligned(i, 2 * block), 2 * block)]
        return dot(part, joined[...], 0, 0).astype(BF16).reshape(buffer.shape[1:])

    def target(i):
        return out_hbm.at[pl.ds(i * block, block)]

    write_blocks(buffer, sems, make, target)


def grad_in(core, own, other, spread):
    both, half = own.shape
    hidden = 2 * half
    width = spread.shape[1] // 2
    block = 128
    steps = width // block
    return pl.pallas_call(
        grad_in_kernel,
        in_specs=[SMEM, VMEM, VMEM, VMEM],
        out_specs=HBM,
        out_shape=shape(width, 2, hidden),
        scratch_shapes=[
            pltpu.VMEM((both, hidden), BF16),
            pltpu.VMEM((steps, block, 2, hidden), BF16),
            pltpu.SemaphoreType.DMA((steps,)),
        ],
        compiler_params=params(24),
        cost_estimate=cost(4 * both * width * hidden, 4 * width * hidden),
    )(core, own, other, spread)


def grad_out_kernel(core_ref, own_ref, other_ref, sc_ref, out_hbm, joined, buffer, sems):
    rows = own_ref.shape[0]
    join_halves(core_ref, own_ref, other_ref, joined)
    block, width = buffer.shape[1:]
    sc = sc_ref[...].reshape(rows, width)

    def make(i):
        return dot(joined[:, pl.ds(aligned(i, block), block)], sc, 0, 0).astype(BF16)

    def target(i):
        return out_hbm.at[pl.ds(aligned(i, block), block)]

    write_blocks(buffer, sems, make, target)


def grad_out(core, own, other, sc_in):
    rows, half = own.shape
    width = sc_in.shape[2]
    block = 256
    steps = 2 * half // block
    return pl.pallas_call(
        grad_out_kernel,
        in_specs=[SMEM, VMEM, VMEM, VMEM],
        out_specs=HBM,
        out_shape=shape(2 * half, width),
        scratch_shapes=[
            pltpu.VMEM((rows, 2 * half), BF16),
            pltpu.VMEM((steps, block, width), BF16),
            pltpu.SemaphoreType.DMA((steps,)),
        ],
        compiler_params=params(24),
        cost_estimate=cost(4 * rows * width * half, 4 * width * half),
    )(core, own, other, sc_in)


def to_tokens_kernel(experts, capacity, routes_ref, gate_ref, cot_ref, rows_hbm, out_ref, grad_ref, dprob_ref, rows, sems):
    width = rows_hbm.shape[2]
    parts = rows_hbm.shape[0] // experts

    def copy(r):
        span = pl.ds(r * experts, experts)
        return pltpu.make_async_copy(rows_hbm.at[span], rows.at[span], sems.at[r])

    for r in range(parts):
        copy(r).start()
    placed, prob = slot_tables(routes_ref, gate_ref, experts, capacity, 2)
    slot = lax.broadcasted_iota(jnp.int32, placed.shape, 0)
    first = slot % (2 * capacity) < capacity
    weight = jnp.where(placed & first, prob, 0.0).astype(BF16)
    place = jnp.where(placed & jnp.logical_not(first), 1.0, 0.0).astype(BF16)
    dots = jnp.zeros(placed.shape, F32)
    for r in range(parts):
        span = slice(r * width, (r + 1) * width)
        copy(r).wait()
        part = rows[r * experts : (r + 1) * experts].reshape(placed.shape[0], width)
        out_ref[:, span] = dot(weight, part, 0, 0).astype(BF16)
        grad_ref[:, span] = dot(place, part, 0, 0).astype(BF16)
        dots = dots + dot(part, cot_ref[:, span], 1, 1)
    dots = jnp.where(placed & first, dots, 0.0)
    expert = slot // (2 * capacity)
    for k in range(dprob_ref.shape[0]):
        term = jnp.where(routes_ref[k : k + 1, :] == expert, dots, 0.0)
        dprob_ref[k : k + 1, :] = jnp.sum(term, axis=0, keepdims=True)


def to_tokens(routes, gate_probs, cotangent, returned, experts, capacity):
    return pl.pallas_call(
        functools.partial(to_tokens_kernel, experts, capacity),
        in_specs=[VMEM, VMEM, VMEM, HBM],
        out_shape=(shape(*cotangent.shape), shape(*cotangent.shape), shape(*routes.shape, dtype=F32)),
        scratch_shapes=[
            pltpu.VMEM(returned.shape, BF16),
            pltpu.SemaphoreType.DMA((returned.shape[0] // experts,)),
        ],
        compiler_params=params(8),
        cost_estimate=cost(6 * returned.size * 8, 2 * returned.size),
    )(routes, gate_probs, cotangent, in_hbm(returned))


def on_device(tokens, routes, gate_probs, cotangent, w_gate_up, w_down):
    n_row = lax.axis_size("erow")
    experts = lax.axis_size("ecol")
    capacity = tokens.shape[0] // 2
    rows = n_row * experts * capacity
    core = (lax.axis_index("erow") % 2).astype(jnp.int32).reshape(1)
    routes, gate_probs = routes.T, gate_probs.T

    x_in = exchange(to_slots(routes, gate_probs, tokens, False, n_row, experts, capacity))
    sc_out = to_slots(routes, gate_probs, cotangent, True, n_row, experts, capacity)
    x_in, sc_out = lax.optimization_barrier((x_in, sc_out))
    sc_in = exchange(sc_out)
    w_in, w_out = w_gate_up[0], w_down[0]

    pre_send, pre_keep, spread = pre_halves(core, x_in, w_in, rows)
    pre_part, pre_others = sum_parts(pre_send, pre_keep)
    hid_send, hid_keep = down_t_halves(core, sc_in, w_out, rows)
    hid_part, hid_others = sum_parts(hid_send, hid_keep)

    pre_others, hid_part = lax.optimization_barrier((pre_others, hid_part))
    pre = total(pre_part, pre_others)
    gate, up = pre[:rows], pre[rows:]
    hidden_own, pre = lax.optimization_barrier(((gate * jax.nn.sigmoid(gate) * up).astype(BF16), pre))
    hidden_other = swap_cores(hidden_own)
    out_rows = expert_out(core, hidden_own, hidden_other, w_out)
    grad_down = grad_out(core, hidden_own, hidden_other, sc_in)[None]

    hid_others, out_rows = lax.optimization_barrier((hid_others, out_rows))
    grad_hidden = total(hid_part, hid_others)
    gate, up = pre[:rows], pre[rows:]
    s = jax.nn.sigmoid(gate)
    activated = gate * s
    grad_gate = grad_hidden * up * s * (1.0 + gate * (1.0 - s))
    grad_up = grad_hidden * activated
    grad_own = jnp.concatenate([grad_gate, grad_up], axis=0).astype(BF16)
    grad_other = swap_cores(grad_own)
    back = exchange(grad_rows(core, grad_own, grad_other, w_in, out_rows, capacity))
    grad_gate_up = grad_in(core, grad_own, grad_other, spread)[None]

    out, grad_tokens, grad_probs = to_tokens(routes, gate_probs, cotangent, back, experts, capacity)
    return (out, grad_tokens, grad_probs.T, grad_gate_up, grad_down)


def solution(mesh):
    flat = P(BOTH, None)
    return jax.shard_map(
        on_device,
        mesh=mesh,
        in_specs=(flat, flat, flat, flat, P("ecol", "erow", None, None), P("ecol", None, "erow")),
        out_specs=(flat, flat, flat, P("ecol", "erow", None, None), P("ecol", None, "erow")),
        check_vma=False,
    )
```

```python
import functools

import jax
import jax.numpy as jnp
from jax import lax
from jax.experimental import pallas as pl
from jax.experimental.pallas import tpu as pltpu
from jax.sharding import PartitionSpec as P

BF16 = jnp.bfloat16
F32 = jnp.float32
BOTH = ("erow", "ecol")
MIB = 1024 * 1024
HBM = pl.BlockSpec(memory_space=pltpu.HBM)
VMEM = pl.BlockSpec(memory_space=pltpu.VMEM)
SMEM = pl.BlockSpec(memory_space=pltpu.SMEM)


def dot(a, b, ca=1, cb=0):
    return lax.dot_general(a, b, (((ca,), (cb,)), ((), ())), preferred_element_type=F32)


def params(mib):
    return pltpu.CompilerParams(vmem_limit_bytes=mib * MIB)


def cost(flops, bytes_accessed):
    return pl.CostEstimate(flops=int(flops), bytes_accessed=int(bytes_accessed), transcendentals=0)


def in_hbm(array):
    return pltpu.with_memory_space_constraint(array, pltpu.HBM)


def shape(*dims, dtype=BF16):
    return jax.ShapeDtypeStruct(dims, dtype)


def aligned(value, step):
    return pl.multiple_of(value * step, step)


def slot_tables(routes_ref, gate_ref, experts, capacity, group=1):
    top, count = routes_ref.shape
    dims = (experts * group * capacity, count)
    slot = lax.broadcasted_iota(jnp.int32, dims, 0)
    expert, rank = slot // (group * capacity), slot % capacity
    member = jnp.zeros(dims, F32)
    prob = jnp.zeros(dims, F32)
    for k in range(top):
        hit = routes_ref[k : k + 1, :] == expert
        member = member + jnp.where(hit, 1.0, 0.0)
        prob = prob + jnp.where(hit, gate_ref[k : k + 1, :].astype(F32), 0.0)
    before = lax.broadcasted_iota(jnp.int32, (count, count), 0)
    after = lax.broadcasted_iota(jnp.int32, (count, count), 1)
    prior = dot(member, jnp.where(before < after, 1.0, 0.0))
    placed = (member > 0.5) & (prior == rank.astype(F32))
    return placed, prob


def slots_kernel(experts, capacity, weighted, routes_hbm, gate_hbm, rows_hbm, out_ref, routes_ref, gate_ref, rows, sems):
    loads = [
        pltpu.make_async_copy(source, target, sems.at[i])
        for i, (source, target) in enumerate(
            ((routes_hbm, routes_ref), (gate_hbm, gate_ref), (rows_hbm, rows))
        )
    ]
    for load in loads:
        load.start()
    loads[0].wait()
    loads[1].wait()
    placed, prob = slot_tables(routes_ref, gate_ref, experts, capacity)
    table = jnp.where(placed, prob if weighted else 1.0, 0.0).astype(BF16)
    loads[2].wait()
    width = out_ref.shape[2]
    for r in range(out_ref.shape[0] // experts):
        part = dot(table, rows[:, r * width : (r + 1) * width]).astype(BF16)
        out_ref[r * experts : (r + 1) * experts] = part.reshape(experts, capacity, width)


def to_slots(routes, gate_probs, rows, weighted, n_row, experts, capacity):
    count, model = rows.shape
    return pl.pallas_call(
        functools.partial(slots_kernel, experts, capacity, weighted),
        in_specs=[HBM, HBM, HBM],
        out_shape=shape(n_row * experts, capacity, model // n_row),
        scratch_shapes=[
            pltpu.VMEM(routes.shape, routes.dtype),
            pltpu.VMEM(gate_probs.shape, BF16),
            pltpu.VMEM(rows.shape, BF16),
            pltpu.SemaphoreType.DMA((3,)),
        ],
        compiler_params=params(8),
        cost_estimate=cost(2 * experts * capacity * count * model, 2 * rows.size),
    )(in_hbm(routes), in_hbm(gate_probs), in_hbm(rows))


def exchange(rows):
    return lax.all_to_all(rows, BOTH, split_axis=0, concat_axis=0, tiled=True)


def stream(copies, ahead=2):
    for copy in copies[:ahead]:
        copy.start()

    def block(i):
        copies[i].wait()
        if i + ahead < len(copies):
            copies[i + ahead].start()

    return block


def spread_rows(x, spread_ref):
    rows, width = x.shape
    d = lax.broadcasted_iota(jnp.int32, (128, 256), 0)
    lane = lax.broadcasted_iota(jnp.int32, (128, 256), 1)
    for g in range(2):
        pattern = jnp.where(lane == 2 * d + g, 1.0, 0.0).astype(BF16)
        for j in range(width // 128):
            part = dot(x[:, j * 128 : (j + 1) * 128], pattern).astype(BF16)
            spread_ref[g * rows : (g + 1) * rows, j * 256 : (j + 1) * 256] = part


def pre_kernel(core_ref, x_ref, w_hbm, send_ref, keep_ref, spread_ref, buffer, sems):
    steps, width, _, block = buffer.shape
    each = steps // 2

    def copy(i):
        part = 1 - core_ref[0] if i < each else core_ref[0]
        source = w_hbm.at[:, :, pl.ds(aligned(part * each + i % each, block), block)]
        return pltpu.make_async_copy(source, buffer.at[i], sems.at[i])

    ready = stream([copy(i) for i in range(steps)])
    spread_rows(x_ref[...].reshape(spread_ref.shape[0] // 2, width), spread_ref)
    for i in range(steps):
        ready(i)
        out_ref = send_ref if i < each else keep_ref
        out = dot(spread_ref[...], buffer[i].reshape(2 * width, block))
        out_ref[:, i % each * block : (i % each + 1) * block] = out.astype(out_ref.dtype)


def pre_halves(core, x_in, w_in, rows):
    width, _, hidden = w_in.shape
    half = hidden // 2
    steps = 4
    return pl.pallas_call(
        pre_kernel,
        in_specs=[SMEM, VMEM, HBM],
        out_specs=[VMEM, VMEM, VMEM],
        out_shape=(
            shape(2 * rows, half),
            shape(2 * rows, half, dtype=F32),
            shape(2 * rows, 2 * width),
        ),
        scratch_shapes=[
            pltpu.VMEM((steps, width, 2, hidden // steps), BF16),
            pltpu.SemaphoreType.DMA((steps,)),
        ],
        compiler_params=params(28),
        cost_estimate=cost(1e10, 4 * width * hidden),
    )(core, x_in, in_hbm(w_in))


def down_t_kernel(core_ref, sc_ref, w_hbm, send_ref, keep_ref, buffer, sems):
    steps, block, width = buffer.shape
    each = steps // 2

    def copy(i):
        part = 1 - core_ref[0] if i < each else core_ref[0]
        source = w_hbm.at[pl.ds(aligned(part * each + i % each, block), block), :]
        return pltpu.make_async_copy(source, buffer.at[i], sems.at[i])

    ready = stream([copy(i) for i in range(steps)])
    sc = sc_ref[...].reshape(send_ref.shape[0], width)
    for i in range(steps):
        ready(i)
        out_ref = send_ref if i < each else keep_ref
        out = dot(sc, buffer[i], 1, 1)
        out_ref[:, i % each * block : (i % each + 1) * block] = out.astype(out_ref.dtype)


def down_t_halves(core, sc_in, w_out, rows):
    hidden, width = w_out.shape
    half = hidden // 2
    steps = 4
    return pl.pallas_call(
        down_t_kernel,
        in_specs=[SMEM, VMEM, HBM],
        out_specs=[VMEM, VMEM],
        out_shape=(shape(rows, half), shape(rows, half, dtype=F32)),
        scratch_shapes=[
            pltpu.VMEM((steps, hidden // steps, width), BF16),
            pltpu.SemaphoreType.DMA((steps,)),
        ],
        compiler_params=params(16),
        cost_estimate=cost(2 * rows * width * hidden, 2 * width * hidden),
    )(core, sc_in, in_hbm(w_out))


def swap_cores(value):
    n_row = lax.axis_size("erow")
    return lax.ppermute(value, "erow", [(i, i ^ 1) for i in range(n_row)])


def sum_parts(send, keep):
    n_row = lax.axis_size("erow")
    pairs = n_row // 2
    chip_sum = (keep + swap_cores(send).astype(F32)).astype(BF16)
    others = []
    for k in range(1, pairs):
        perm = [(i, ((i // 2 + k) % pairs) * 2 + i % 2) for i in range(n_row)]
        others.append(lax.ppermute(chip_sum, "erow", perm))
    return chip_sum, others


def total(part, others):
    out = part.astype(F32)
    for other in others:
        out = out + other.astype(F32)
    return out


def hidden_kernel(*refs):
    rows = refs[-1].shape[0]
    pre = refs[0][...].astype(F32)
    for ref in refs[1:-1]:
        pre = pre + ref[...].astype(F32)
    gate, up = pre[:rows], pre[rows:]
    refs[-1][...] = (gate * jax.nn.sigmoid(gate) * up).astype(BF16)


def hidden_half(part, others):
    both, half = part.shape
    return pl.pallas_call(
        hidden_kernel,
        out_shape=shape(both // 2, half),
        compiler_params=params(6),
        cost_estimate=cost(6 * part.size, 4 * part.size),
    )(part, *others)


def expert_out_kernel(spans, core_ref, own_ref, other_ref, w_hbm, out_ref, joined, buffer, sems):
    copies = [
        pltpu.make_async_copy(w_hbm.at[:, pl.ds(at, size)], buffer.at[:, pl.ds(at, size)], sems.at[i])
        for i, (at, size) in enumerate(spans)
    ]
    ready = stream(copies)
    join_halves(core_ref, own_ref, other_ref, joined)
    for i, (at, size) in enumerate(spans):
        ready(i)
        out_ref[:, at : at + size] = dot(joined[...], buffer[:, at : at + size]).astype(BF16)


def expert_out(core, own, other, w_out):
    rows, half = own.shape
    hidden, width = w_out.shape
    edges = [width // 128 * i // 4 * 128 for i in range(5)]
    spans = [(at, to - at) for at, to in zip(edges, edges[1:])]
    return pl.pallas_call(
        functools.partial(expert_out_kernel, spans),
        in_specs=[SMEM, VMEM, VMEM, HBM],
        out_specs=VMEM,
        out_shape=shape(rows, width),
        scratch_shapes=[
            pltpu.VMEM((rows, hidden), BF16),
            pltpu.VMEM((hidden, width), BF16),
            pltpu.SemaphoreType.DMA((len(spans),)),
        ],
        compiler_params=params(16),
        cost_estimate=cost(5e9, 2 * width * hidden),
    )(core, own, other, in_hbm(w_out))


def join_halves(core_ref, own_ref, other_ref, joined):
    half = own_ref.shape[1]
    joined[:, pl.ds(aligned(core_ref[0], half), half)] = own_ref[...]
    joined[:, pl.ds(aligned(1 - core_ref[0], half), half)] = other_ref[...]


def grad_rows_kernel(steps, core_ref, own_ref, other_ref, w_ref, eo_ref, out_ref, joined, product):
    join_halves(core_ref, own_ref, other_ref, joined)
    rows = eo_ref.shape[0]
    width, _, hidden = w_ref.shape
    block = width // steps
    capacity = out_ref.shape[1] // 2
    chunks = rows // 128
    for i in range(steps):
        span = slice(i * block, (i + 1) * block)
        out = dot(w_ref[span].reshape(2 * block, hidden), joined[...], 1, 1)
        for j in range(2 * chunks):
            product[i % 2, j] = out[:, j * 128 : (j + 1) * 128]
        for j in range(chunks):
            gate = product[i % 2, j, pl.ds(0, block, stride=2), :]
            up = product[i % 2, chunks + j, pl.ds(1, block, stride=2), :]
            turned = (gate + up).T.astype(BF16).reshape(128 // capacity, capacity, block)
            kept = eo_ref[j * 128 : (j + 1) * 128, span].reshape(128 // capacity, capacity, block)
            both = jnp.concatenate([kept, turned], axis=1)
            out_ref[j * 128 // capacity : (j + 1) * 128 // capacity, :, span] = both


def grad_rows(core, own, other, w_in, out_rows, capacity):
    rows, width = out_rows.shape
    hidden = w_in.shape[2]
    steps = 7
    block = width // steps
    return pl.pallas_call(
        functools.partial(grad_rows_kernel, steps),
        in_specs=[SMEM, VMEM, VMEM, VMEM, VMEM],
        out_specs=VMEM,
        out_shape=shape(rows // capacity, 2 * capacity, width),
        scratch_shapes=[
            pltpu.VMEM((2 * rows, hidden), BF16),
            pltpu.VMEM((2, 2 * rows // 128, 2 * block, 128), F32),
        ],
        compiler_params=params(16),
        cost_estimate=cost(8 * rows * width * hidden, 4 * width * hidden),
    )(core, own, other, w_in, out_rows)


def write_blocks(buffer, sems, make, target):
    steps = buffer.shape[0]

    def copy(i):
        return pltpu.make_async_copy(buffer.at[i], target(i), sems.at[i])

    @pl.loop(0, steps)
    def _(i):
        buffer[i] = make(i)
        copy(i).start()

    @pl.loop(0, steps)
    def _(i):
        copy(i).wait()


def grad_in_kernel(core_ref, own_ref, other_ref, spread_ref, out_hbm, joined, buffer, sems):
    join_halves(core_ref, own_ref, other_ref, joined)
    block = buffer.shape[1]

    def make(i):
        part = spread_ref[:, pl.ds(aligned(i, 2 * block), 2 * block)]
        return dot(part, joined[...], 0, 0).astype(BF16).reshape(buffer.shape[1:])

    def target(i):
        return out_hbm.at[pl.ds(i * block, block)]

    write_blocks(buffer, sems, make, target)


def grad_in(core, own, other, spread):
    both, half = own.shape
    hidden = 2 * half
    width = spread.shape[1] // 2
    block = 128
    steps = width // block
    return pl.pallas_call(
        grad_in_kernel,
        in_specs=[SMEM, VMEM, VMEM, VMEM],
        out_specs=HBM,
        out_shape=shape(width, 2, hidden),
        scratch_shapes=[
            pltpu.VMEM((both, hidden), BF16),
            pltpu.VMEM((steps, block, 2, hidden), BF16),
            pltpu.SemaphoreType.DMA((steps,)),
        ],
        compiler_params=params(24),
        cost_estimate=cost(4 * both * width * hidden, 4 * width * hidden),
    )(core, own, other, spread)


def grad_out_kernel(core_ref, own_ref, other_ref, sc_ref, out_hbm, joined, buffer, sems):
    rows = own_ref.shape[0]
    join_halves(core_ref, own_ref, other_ref, joined)
    block, width = buffer.shape[1:]
    sc = sc_ref[...].reshape(rows, width)

    def make(i):
        return dot(joined[:, pl.ds(aligned(i, block), block)], sc, 0, 0).astype(BF16)

    def target(i):
        return out_hbm.at[pl.ds(aligned(i, block), block)]

    write_blocks(buffer, sems, make, target)


def grad_out(core, own, other, sc_in):
    rows, half = own.shape
    width = sc_in.shape[2]
    block = 256
    steps = 2 * half // block
    return pl.pallas_call(
        grad_out_kernel,
        in_specs=[SMEM, VMEM, VMEM, VMEM],
        out_specs=HBM,
        out_shape=shape(2 * half, width),
        scratch_shapes=[
            pltpu.VMEM((rows, 2 * half), BF16),
            pltpu.VMEM((steps, block, width), BF16),
            pltpu.SemaphoreType.DMA((steps,)),
        ],
        compiler_params=params(24),
        cost_estimate=cost(4 * rows * width * half, 4 * width * half),
    )(core, own, other, sc_in)


def to_tokens_kernel(experts, capacity, routes_ref, gate_ref, cot_ref, rows_hbm, out_ref, grad_ref, dprob_ref, rows, sems):
    width = rows_hbm.shape[2]
    parts = rows_hbm.shape[0] // experts

    def copy(r):
        span = pl.ds(r * experts, experts)
        return pltpu.make_async_copy(rows_hbm.at[span], rows.at[span], sems.at[r])

    for r in range(parts):
        copy(r).start()
    placed, prob = slot_tables(routes_ref, gate_ref, experts, capacity, 2)
    slot = lax.broadcasted_iota(jnp.int32, placed.shape, 0)
    first = slot % (2 * capacity) < capacity
    weight = jnp.where(placed & first, prob, 0.0).astype(BF16)
    place = jnp.where(placed & jnp.logical_not(first), 1.0, 0.0).astype(BF16)
    dots = jnp.zeros(placed.shape, F32)
    for r in range(parts):
        span = slice(r * width, (r + 1) * width)
        copy(r).wait()
        part = rows[r * experts : (r + 1) * experts].reshape(placed.shape[0], width)
        out_ref[:, span] = dot(weight, part, 0, 0).astype(BF16)
        grad_ref[:, span] = dot(place, part, 0, 0).astype(BF16)
        dots = dots + dot(part, cot_ref[:, span], 1, 1)
    dots = jnp.where(placed & first, dots, 0.0)
    expert = slot // (2 * capacity)
    for k in range(dprob_ref.shape[0]):
        term = jnp.where(routes_ref[k : k + 1, :] == expert, dots, 0.0)
        dprob_ref[k : k + 1, :] = jnp.sum(term, axis=0, keepdims=True)


def to_tokens(routes, gate_probs, cotangent, returned, experts, capacity):
    return pl.pallas_call(
        functools.partial(to_tokens_kernel, experts, capacity),
        in_specs=[VMEM, VMEM, VMEM, HBM],
        out_shape=(shape(*cotangent.shape), shape(*cotangent.shape), shape(*routes.shape, dtype=F32)),
        scratch_shapes=[
            pltpu.VMEM(returned.shape, BF16),
            pltpu.SemaphoreType.DMA((returned.shape[0] // experts,)),
        ],
        compiler_params=params(8),
        cost_estimate=cost(6 * returned.size * 8, 2 * returned.size),
    )(routes, gate_probs, cotangent, in_hbm(returned))


def on_device(tokens, routes, gate_probs, cotangent, w_gate_up, w_down):
    n_row = lax.axis_size("erow")
    experts = lax.axis_size("ecol")
    capacity = tokens.shape[0] // 2
    rows = n_row * experts * capacity
    core = (lax.axis_index("erow") % 2).astype(jnp.int32).reshape(1)
    routes, gate_probs = routes.T, gate_probs.T

    x_in = exchange(to_slots(routes, gate_probs, tokens, False, n_row, experts, capacity))
    sc_out = to_slots(routes, gate_probs, cotangent, True, n_row, experts, capacity)
    x_in, sc_out = lax.optimization_barrier((x_in, sc_out))
    sc_in = exchange(sc_out)
    w_in, w_out = w_gate_up[0], w_down[0]

    pre_send, pre_keep, spread = pre_halves(core, x_in, w_in, rows)
    pre_part, pre_others = sum_parts(pre_send, pre_keep)
    hid_send, hid_keep = down_t_halves(core, sc_in, w_out, rows)
    hid_part, hid_others = sum_parts(hid_send, hid_keep)

    pre_others, hid_part = lax.optimization_barrier((pre_others, hid_part))
    hidden_own = hidden_half(pre_part, pre_others)
    hidden_other = swap_cores(hidden_own)
    out_rows = expert_out(core, hidden_own, hidden_other, w_out)
    grad_down = grad_out(core, hidden_own, hidden_other, sc_in)[None]

    hid_others, out_rows = lax.optimization_barrier((hid_others, out_rows))
    grad_hidden = total(hid_part, hid_others)
    pre = total(pre_part, pre_others)
    gate, up = pre[:rows], pre[rows:]
    s = jax.nn.sigmoid(gate)
    activated = gate * s
    grad_gate = grad_hidden * up * s * (1.0 + gate * (1.0 - s))
    grad_up = grad_hidden * activated
    grad_own = jnp.concatenate([grad_gate, grad_up], axis=0).astype(BF16)
    grad_other = swap_cores(grad_own)
    back = exchange(grad_rows(core, grad_own, grad_other, w_in, out_rows, capacity))
    grad_gate_up = grad_in(core, grad_own, grad_other, spread)[None]

    out, grad_tokens, grad_probs = to_tokens(routes, gate_probs, cotangent, back, experts, capacity)
    return (out, grad_tokens, grad_probs.T, grad_gate_up, grad_down)


def solution(mesh):
    flat = P(BOTH, None)
    return jax.shard_map(
        on_device,
        mesh=mesh,
        in_specs=(flat, flat, flat, flat, P("ecol", "erow", None, None), P("ecol", None, "erow")),
        out_specs=(flat, flat, flat, P("ecol", "erow", None, None), P("ecol", None, "erow")),
        check_vma=False,
    )
```

```python
import functools

import jax
import jax.numpy as jnp
from jax import lax
from jax.experimental import pallas as pl
from jax.experimental.pallas import tpu as pltpu
from jax.sharding import PartitionSpec as P

BF16 = jnp.bfloat16
F32 = jnp.float32
BOTH = ("erow", "ecol")
MIB = 1024 * 1024
HBM = pl.BlockSpec(memory_space=pltpu.HBM)
VMEM = pl.BlockSpec(memory_space=pltpu.VMEM)
SMEM = pl.BlockSpec(memory_space=pltpu.SMEM)


def dot(a, b, ca=1, cb=0):
    return lax.dot_general(a, b, (((ca,), (cb,)), ((), ())), preferred_element_type=F32)


def params(mib):
    return pltpu.CompilerParams(vmem_limit_bytes=mib * MIB)


def cost(flops, bytes_accessed):
    return pl.CostEstimate(flops=int(flops), bytes_accessed=int(bytes_accessed), transcendentals=0)


def in_hbm(array):
    return pltpu.with_memory_space_constraint(array, pltpu.HBM)


def shape(*dims, dtype=BF16):
    return jax.ShapeDtypeStruct(dims, dtype)


def aligned(value, step):
    return pl.multiple_of(value * step, step)


def slot_tables(routes_ref, gate_ref, experts, capacity, group=1):
    top, count = routes_ref.shape
    dims = (experts * group * capacity, count)
    slot = lax.broadcasted_iota(jnp.int32, dims, 0)
    expert, rank = slot // (group * capacity), slot % capacity
    member = jnp.zeros(dims, F32)
    prob = jnp.zeros(dims, F32)
    for k in range(top):
        hit = routes_ref[k : k + 1, :] == expert
        member = member + jnp.where(hit, 1.0, 0.0)
        prob = prob + jnp.where(hit, gate_ref[k : k + 1, :].astype(F32), 0.0)
    before = lax.broadcasted_iota(jnp.int32, (count, count), 0)
    after = lax.broadcasted_iota(jnp.int32, (count, count), 1)
    prior = dot(member, jnp.where(before < after, 1.0, 0.0))
    placed = (member > 0.5) & (prior == rank.astype(F32))
    return placed, prob


def slots_kernel(experts, capacity, weighted, routes_hbm, gate_hbm, rows_hbm, out_ref, routes_ref, gate_ref, rows, sems):
    loads = [
        pltpu.make_async_copy(source, target, sems.at[i])
        for i, (source, target) in enumerate(
            ((routes_hbm, routes_ref), (gate_hbm, gate_ref), (rows_hbm, rows))
        )
    ]
    for load in loads:
        load.start()
    loads[0].wait()
    loads[1].wait()
    placed, prob = slot_tables(routes_ref, gate_ref, experts, capacity)
    table = jnp.where(placed, prob if weighted else 1.0, 0.0).astype(BF16)
    loads[2].wait()
    width = out_ref.shape[2]
    for r in range(out_ref.shape[0] // experts):
        part = dot(table, rows[:, r * width : (r + 1) * width]).astype(BF16)
        out_ref[r * experts : (r + 1) * experts] = part.reshape(experts, capacity, width)


def to_slots(routes, gate_probs, rows, weighted, n_row, experts, capacity):
    count, model = rows.shape
    return pl.pallas_call(
        functools.partial(slots_kernel, experts, capacity, weighted),
        in_specs=[HBM, HBM, HBM],
        out_shape=shape(n_row * experts, capacity, model // n_row),
        scratch_shapes=[
            pltpu.VMEM(routes.shape, routes.dtype),
            pltpu.VMEM(gate_probs.shape, BF16),
            pltpu.VMEM(rows.shape, BF16),
            pltpu.SemaphoreType.DMA((3,)),
        ],
        compiler_params=params(8),
        cost_estimate=cost(2 * experts * capacity * count * model, 2 * rows.size),
    )(in_hbm(routes), in_hbm(gate_probs), in_hbm(rows))


def exchange(rows):
    return lax.all_to_all(rows, BOTH, split_axis=0, concat_axis=0, tiled=True)


def stream(copies, ahead=4):
    for copy in copies[:ahead]:
        copy.start()

    def block(i):
        copies[i].wait()
        if i + ahead < len(copies):
            copies[i + ahead].start()

    return block


def spread_rows(x, spread_ref):
    rows, width = x.shape
    d = lax.broadcasted_iota(jnp.int32, (128, 256), 0)
    lane = lax.broadcasted_iota(jnp.int32, (128, 256), 1)
    for g in range(2):
        pattern = jnp.where(lane == 2 * d + g, 1.0, 0.0).astype(BF16)
        for j in range(width // 128):
            part = dot(x[:, j * 128 : (j + 1) * 128], pattern).astype(BF16)
            spread_ref[g * rows : (g + 1) * rows, j * 256 : (j + 1) * 256] = part


def pre_kernel(core_ref, x_ref, w_hbm, send_ref, keep_ref, spread_ref, buffer, sems):
    steps, width, _, block = buffer.shape
    each = steps // 2

    def copy(i):
        part = 1 - core_ref[0] if i < each else core_ref[0]
        source = w_hbm.at[:, :, pl.ds(aligned(part * each + i % each, block), block)]
        return pltpu.make_async_copy(source, buffer.at[i], sems.at[i])

    ready = stream([copy(i) for i in range(steps)])
    spread_rows(x_ref[...].reshape(spread_ref.shape[0] // 2, width), spread_ref)
    for i in range(steps):
        ready(i)
        out_ref = send_ref if i < each else keep_ref
        out = dot(spread_ref[...], buffer[i].reshape(2 * width, block))
        out_ref[:, i % each * block : (i % each + 1) * block] = out.astype(out_ref.dtype)


def pre_halves(core, x_in, w_in, rows):
    width, _, hidden = w_in.shape
    half = hidden // 2
    steps = 4
    return pl.pallas_call(
        pre_kernel,
        in_specs=[SMEM, VMEM, HBM],
        out_specs=[VMEM, VMEM, VMEM],
        out_shape=(
            shape(2 * rows, half),
            shape(2 * rows, half, dtype=F32),
            shape(2 * rows, 2 * width),
        ),
        scratch_shapes=[
            pltpu.VMEM((steps, width, 2, hidden // steps), BF16),
            pltpu.SemaphoreType.DMA((steps,)),
        ],
        compiler_params=params(28),
        cost_estimate=cost(1e10, 4 * width * hidden),
    )(core, x_in, in_hbm(w_in))


def down_t_kernel(core_ref, sc_ref, w_hbm, send_ref, keep_ref, buffer, sems):
    steps, block, width = buffer.shape
    each = steps // 2

    def copy(i):
        part = 1 - core_ref[0] if i < each else core_ref[0]
        source = w_hbm.at[pl.ds(aligned(part * each + i % each, block), block), :]
        return pltpu.make_async_copy(source, buffer.at[i], sems.at[i])

    ready = stream([copy(i) for i in range(steps)])
    sc = sc_ref[...].reshape(send_ref.shape[0], width)
    for i in range(steps):
        ready(i)
        out_ref = send_ref if i < each else keep_ref
        out = dot(sc, buffer[i], 1, 1)
        out_ref[:, i % each * block : (i % each + 1) * block] = out.astype(out_ref.dtype)


def down_t_halves(core, sc_in, w_out, rows):
    hidden, width = w_out.shape
    half = hidden // 2
    steps = 4
    return pl.pallas_call(
        down_t_kernel,
        in_specs=[SMEM, VMEM, HBM],
        out_specs=[VMEM, VMEM],
        out_shape=(shape(rows, half), shape(rows, half, dtype=F32)),
        scratch_shapes=[
            pltpu.VMEM((steps, hidden // steps, width), BF16),
            pltpu.SemaphoreType.DMA((steps,)),
        ],
        compiler_params=params(16),
        cost_estimate=cost(2 * rows * width * hidden, 2 * width * hidden),
    )(core, sc_in, in_hbm(w_out))


def swap_cores(value):
    n_row = lax.axis_size("erow")
    return lax.ppermute(value, "erow", [(i, i ^ 1) for i in range(n_row)])


def sum_parts(send, keep):
    n_row = lax.axis_size("erow")
    pairs = n_row // 2
    chip_sum = (keep + swap_cores(send).astype(F32)).astype(BF16)
    others = []
    for k in range(1, pairs):
        perm = [(i, ((i // 2 + k) % pairs) * 2 + i % 2) for i in range(n_row)]
        others.append(lax.ppermute(chip_sum, "erow", perm))
    return chip_sum, others


def total(part, others):
    out = part.astype(F32)
    for other in others:
        out = out + other.astype(F32)
    return out


def hidden_kernel(*refs):
    rows = refs[-1].shape[0]
    pre = refs[0][...].astype(F32)
    for ref in refs[1:-1]:
        pre = pre + ref[...].astype(F32)
    gate, up = pre[:rows], pre[rows:]
    refs[-1][...] = (gate * jax.nn.sigmoid(gate) * up).astype(BF16)


def hidden_half(part, others):
    both, half = part.shape
    return pl.pallas_call(
        hidden_kernel,
        out_shape=shape(both // 2, half),
        compiler_params=params(6),
        cost_estimate=cost(6 * part.size, 4 * part.size),
    )(part, *others)


def expert_out_kernel(spans, core_ref, own_ref, other_ref, w_hbm, out_ref, joined, buffer, sems):
    copies = [
        pltpu.make_async_copy(w_hbm.at[:, pl.ds(at, size)], buffer.at[:, pl.ds(at, size)], sems.at[i])
        for i, (at, size) in enumerate(spans)
    ]
    ready = stream(copies)
    join_halves(core_ref, own_ref, other_ref, joined)
    for i, (at, size) in enumerate(spans):
        ready(i)
        out_ref[:, at : at + size] = dot(joined[...], buffer[:, at : at + size]).astype(BF16)


def expert_out(core, own, other, w_out):
    rows, half = own.shape
    hidden, width = w_out.shape
    edges = [width // 128 * i // 4 * 128 for i in range(5)]
    spans = [(at, to - at) for at, to in zip(edges, edges[1:])]
    return pl.pallas_call(
        functools.partial(expert_out_kernel, spans),
        in_specs=[SMEM, VMEM, VMEM, HBM],
        out_specs=VMEM,
        out_shape=shape(rows, width),
        scratch_shapes=[
            pltpu.VMEM((rows, hidden), BF16),
            pltpu.VMEM((hidden, width), BF16),
            pltpu.SemaphoreType.DMA((len(spans),)),
        ],
        compiler_params=params(16),
        cost_estimate=cost(5e9, 2 * width * hidden),
    )(core, own, other, in_hbm(w_out))


def join_halves(core_ref, own_ref, other_ref, joined):
    half = own_ref.shape[1]
    joined[:, pl.ds(aligned(core_ref[0], half), half)] = own_ref[...]
    joined[:, pl.ds(aligned(1 - core_ref[0], half), half)] = other_ref[...]


def grad_rows_kernel(steps, core_ref, own_ref, other_ref, w_ref, eo_ref, out_ref, joined, product):
    join_halves(core_ref, own_ref, other_ref, joined)
    rows = eo_ref.shape[0]
    width, _, hidden = w_ref.shape
    block = width // steps
    capacity = out_ref.shape[1] // 2
    chunks = rows // 128
    for i in range(steps):
        span = slice(i * block, (i + 1) * block)
        out = dot(w_ref[span].reshape(2 * block, hidden), joined[...], 1, 1)
        for j in range(2 * chunks):
            product[i % 2, j] = out[:, j * 128 : (j + 1) * 128]
        for j in range(chunks):
            gate = product[i % 2, j, pl.ds(0, block, stride=2), :]
            up = product[i % 2, chunks + j, pl.ds(1, block, stride=2), :]
            turned = (gate + up).T.astype(BF16).reshape(128 // capacity, capacity, block)
            kept = eo_ref[j * 128 : (j + 1) * 128, span].reshape(128 // capacity, capacity, block)
            both = jnp.concatenate([kept, turned], axis=1)
            out_ref[j * 128 // capacity : (j + 1) * 128 // capacity, :, span] = both


def grad_rows(core, own, other, w_in, out_rows, capacity):
    rows, width = out_rows.shape
    hidden = w_in.shape[2]
    steps = 7
    block = width // steps
    return pl.pallas_call(
        functools.partial(grad_rows_kernel, steps),
        in_specs=[SMEM, VMEM, VMEM, VMEM, VMEM],
        out_specs=VMEM,
        out_shape=shape(rows // capacity, 2 * capacity, width),
        scratch_shapes=[
            pltpu.VMEM((2 * rows, hidden), BF16),
            pltpu.VMEM((2, 2 * rows // 128, 2 * block, 128), F32),
        ],
        compiler_params=params(16),
        cost_estimate=cost(8 * rows * width * hidden, 4 * width * hidden),
    )(core, own, other, w_in, out_rows)


def write_blocks(buffer, sems, make, target):
    steps = buffer.shape[0]

    def copy(i):
        return pltpu.make_async_copy(buffer.at[i], target(i), sems.at[i])

    @pl.loop(0, steps)
    def _(i):
        buffer[i] = make(i)
        copy(i).start()

    @pl.loop(0, steps)
    def _(i):
        copy(i).wait()


def grad_in_kernel(core_ref, own_ref, other_ref, spread_ref, out_hbm, joined, buffer, sems):
    join_halves(core_ref, own_ref, other_ref, joined)
    block = buffer.shape[1]

    def make(i):
        part = spread_ref[:, pl.ds(aligned(i, 2 * block), 2 * block)]
        return dot(part, joined[...], 0, 0).astype(BF16).reshape(buffer.shape[1:])

    def target(i):
        return out_hbm.at[pl.ds(i * block, block)]

    write_blocks(buffer, sems, make, target)


def grad_in(core, own, other, spread):
    both, half = own.shape
    hidden = 2 * half
    width = spread.shape[1] // 2
    block = 128
    steps = width // block
    return pl.pallas_call(
        grad_in_kernel,
        in_specs=[SMEM, VMEM, VMEM, VMEM],
        out_specs=HBM,
        out_shape=shape(width, 2, hidden),
        scratch_shapes=[
            pltpu.VMEM((both, hidden), BF16),
            pltpu.VMEM((steps, block, 2, hidden), BF16),
            pltpu.SemaphoreType.DMA((steps,)),
        ],
        compiler_params=params(24),
        cost_estimate=cost(4 * both * width * hidden, 4 * width * hidden),
    )(core, own, other, spread)


def grad_out_kernel(core_ref, own_ref, other_ref, sc_ref, out_hbm, joined, buffer, sems):
    rows = own_ref.shape[0]
    join_halves(core_ref, own_ref, other_ref, joined)
    block, width = buffer.shape[1:]
    sc = sc_ref[...].reshape(rows, width)

    def make(i):
        return dot(joined[:, pl.ds(aligned(i, block), block)], sc, 0, 0).astype(BF16)

    def target(i):
        return out_hbm.at[pl.ds(aligned(i, block), block)]

    write_blocks(buffer, sems, make, target)


def grad_out(core, own, other, sc_in):
    rows, half = own.shape
    width = sc_in.shape[2]
    block = 256
    steps = 2 * half // block
    return pl.pallas_call(
        grad_out_kernel,
        in_specs=[SMEM, VMEM, VMEM, VMEM],
        out_specs=HBM,
        out_shape=shape(2 * half, width),
        scratch_shapes=[
            pltpu.VMEM((rows, 2 * half), BF16),
            pltpu.VMEM((steps, block, width), BF16),
            pltpu.SemaphoreType.DMA((steps,)),
        ],
        compiler_params=params(24),
        cost_estimate=cost(4 * rows * width * half, 4 * width * half),
    )(core, own, other, sc_in)


def to_tokens_kernel(experts, capacity, routes_ref, gate_ref, cot_ref, rows_hbm, out_ref, grad_ref, dprob_ref, rows, sems):
    width = rows_hbm.shape[2]
    parts = rows_hbm.shape[0] // experts

    def copy(r):
        span = pl.ds(r * experts, experts)
        return pltpu.make_async_copy(rows_hbm.at[span], rows.at[span], sems.at[r])

    for r in range(parts):
        copy(r).start()
    placed, prob = slot_tables(routes_ref, gate_ref, experts, capacity, 2)
    slot = lax.broadcasted_iota(jnp.int32, placed.shape, 0)
    first = slot % (2 * capacity) < capacity
    weight = jnp.where(placed & first, prob, 0.0).astype(BF16)
    place = jnp.where(placed & jnp.logical_not(first), 1.0, 0.0).astype(BF16)
    dots = jnp.zeros(placed.shape, F32)
    for r in range(parts):
        span = slice(r * width, (r + 1) * width)
        copy(r).wait()
        part = rows[r * experts : (r + 1) * experts].reshape(placed.shape[0], width)
        out_ref[:, span] = dot(weight, part, 0, 0).astype(BF16)
        grad_ref[:, span] = dot(place, part, 0, 0).astype(BF16)
        dots = dots + dot(part, cot_ref[:, span], 1, 1)
    dots = jnp.where(placed & first, dots, 0.0)
    expert = slot // (2 * capacity)
    for k in range(dprob_ref.shape[0]):
        term = jnp.where(routes_ref[k : k + 1, :] == expert, dots, 0.0)
        dprob_ref[k : k + 1, :] = jnp.sum(term, axis=0, keepdims=True)


def to_tokens(routes, gate_probs, cotangent, returned, experts, capacity):
    return pl.pallas_call(
        functools.partial(to_tokens_kernel, experts, capacity),
        in_specs=[VMEM, VMEM, VMEM, HBM],
        out_shape=(shape(*cotangent.shape), shape(*cotangent.shape), shape(*routes.shape, dtype=F32)),
        scratch_shapes=[
            pltpu.VMEM(returned.shape, BF16),
            pltpu.SemaphoreType.DMA((returned.shape[0] // experts,)),
        ],
        compiler_params=params(8),
        cost_estimate=cost(6 * returned.size * 8, 2 * returned.size),
    )(routes, gate_probs, cotangent, in_hbm(returned))


def on_device(tokens, routes, gate_probs, cotangent, w_gate_up, w_down):
    n_row = lax.axis_size("erow")
    experts = lax.axis_size("ecol")
    capacity = tokens.shape[0] // 2
    rows = n_row * experts * capacity
    core = (lax.axis_index("erow") % 2).astype(jnp.int32).reshape(1)
    routes, gate_probs = routes.T, gate_probs.T

    x_in = exchange(to_slots(routes, gate_probs, tokens, False, n_row, experts, capacity))
    sc_out = to_slots(routes, gate_probs, cotangent, True, n_row, experts, capacity)
    x_in, sc_out = lax.optimization_barrier((x_in, sc_out))
    sc_in = exchange(sc_out)
    w_in, w_out = w_gate_up[0], w_down[0]

    pre_send, pre_keep, spread = pre_halves(core, x_in, w_in, rows)
    pre_part, pre_others = sum_parts(pre_send, pre_keep)
    hid_send, hid_keep = down_t_halves(core, sc_in, w_out, rows)
    hid_part, hid_others = sum_parts(hid_send, hid_keep)

    pre_others, hid_part = lax.optimization_barrier((pre_others, hid_part))
    hidden_own = hidden_half(pre_part, pre_others)
    hidden_other = swap_cores(hidden_own)
    out_rows = expert_out(core, hidden_own, hidden_other, w_out)
    grad_down = grad_out(core, hidden_own, hidden_other, sc_in)[None]

    hid_others, out_rows = lax.optimization_barrier((hid_others, out_rows))
    grad_hidden = total(hid_part, hid_others)
    pre = total(pre_part, pre_others)
    gate, up = pre[:rows], pre[rows:]
    s = jax.nn.sigmoid(gate)
    activated = gate * s
    grad_gate = grad_hidden * up * s * (1.0 + gate * (1.0 - s))
    grad_up = grad_hidden * activated
    grad_own = jnp.concatenate([grad_gate, grad_up], axis=0).astype(BF16)
    grad_other = swap_cores(grad_own)
    back = exchange(grad_rows(core, grad_own, grad_other, w_in, out_rows, capacity))
    grad_gate_up = grad_in(core, grad_own, grad_other, spread)[None]

    out, grad_tokens, grad_probs = to_tokens(routes, gate_probs, cotangent, back, experts, capacity)
    return (out, grad_tokens, grad_probs.T, grad_gate_up, grad_down)


def solution(mesh):
    flat = P(BOTH, None)
    return jax.shard_map(
        on_device,
        mesh=mesh,
        in_specs=(flat, flat, flat, flat, P("ecol", "erow", None, None), P("ecol", None, "erow")),
        out_specs=(flat, flat, flat, P("ecol", "erow", None, None), P("ecol", None, "erow")),
        check_vma=False,
    )
```
